32 devices in a mesh: grp: 4 (over z), lane: 8 (over y, x, core).
Axes of the slice: x: 2, y: 2, z: 4, core: 2. Of those that a mesh axis runs over, the one named last changes fastest.
Arguments:
- tokens: bfloat16 [64, 7168], P('grp', 'lane'), may hold values from -6 to 6
- grad_out: bfloat16 [64, 7168], P('grp', 'lane'), may hold values from -6 to 6
- routes: int32 [64, 2], P('grp'), may hold values from 0 to 3, all different within a row; in each aligned block of 16 rows (0 to 15, 16 to 31, ...) at most 8 rows name the same one
- route_probs: bfloat16 [64, 2], P('grp'), may hold values from 0.049804688 to 1
- gate_weight: bfloat16 [4, 7168, 1024], P('grp', 'lane'), may hold values from -0.0625 to 0.0625
- up_weight: bfloat16 [4, 7168, 1024], P('grp', 'lane'), may hold values from -0.0625 to 0.0625
- down_weight: bfloat16 [4, 1024, 7168], P('grp', None, 'lane'), may hold values from -0.0625 to 0.0625
Outputs:
- token_grad: bfloat16 [64, 7168], P('grp', 'lane')
- prob_grad: bfloat16 [64, 2], P('grp')
- gate_grad: bfloat16 [4, 7168, 1024], P('grp', 'lane')
- up_grad: bfloat16 [4, 7168, 1024], P('grp', 'lane')
- down_grad: bfloat16 [4, 1024, 7168], P('grp', None, 'lane')
The draws below stay inside these ranges and needn't reach their ends.
Inputs may be any that keep to these rules, and one draw needn't show every extreme that they name: `routes`: each row names 2 different experts. Among the 16 rows of one index of grp (aligned blocks of rows), no expert is named by more than 8 rows, a bound that some block reaches.
All inputs are finite; a program needn't handle non-finite values.
Results may differ from the reference program's by a relative error of at most 0.023.
Values may be sent and summed in bfloat16 or wider, within the bound.
A program may use at most 64 MiB of HBM per device.

```python
import math
import jax
import jax.numpy as jnp
import numpy as np
from jax import lax

D = 7168
UNITS = 1024
TOK_GRP = 16
MOST = 8
EXPERTS = 4
TOP = 2
TOKENS = 64
N_LANE = 8


def block_levels(stream_key, dims, shards, low, high):
    gain, own = 1.0, jax.random.fold_in(stream_key, 6)
    for axis_at, blocks in shards:
        heights = jnp.exp(jax.random.uniform(jax.random.fold_in(own, axis_at), (blocks,), jnp.float32, low / len(shards), high / len(shards)))
        gain = gain * jnp.repeat(heights, dims[axis_at] // blocks).reshape([-1 if axis == axis_at else 1 for axis in range(len(dims))])
    return gain


def routed_block(rng, own, number, rows, count, top, bound, skew):
    ranking = jax.random.permutation(rng, count)
    packed, usual = portions_of(count, rows * top, bound, skew, True), portions_of(count, rows * top, bound, skew, False)
    places = jnp.arange(count)

    def named(lengths, offset_by):
        used = int((lengths > 0).sum())
        fixed = max(1, used // 4)
        passed = fixed + (places - fixed + offset_by * (used - fixed)) % max(1, count - fixed)
        return jnp.zeros((count,), jnp.int32).at[ranking[jnp.where(places < fixed, places, passed)]].set(jnp.asarray(lengths, jnp.int32))

    lengths = jnp.where(number % 4 == 0, named(packed, number // 4), named(usual, number - number // 4 - 1))
    mixed = jax.random.permutation(jax.random.fold_in(own, 3), count)
    giver, sink = mixed[0:count // 2 * 2:2], mixed[1:count // 2 * 2:2]
    margin = jnp.minimum(lengths[giver] - 1, bound - lengths[sink]) // 2
    margin = jnp.where((giver == ranking[0]) | (sink == ranking[0]) | (lengths[sink] == 0), 0, jnp.maximum(margin, 0))
    passed = jax.random.randint(jax.random.fold_in(own, 4), (count // 2,), 0, 1 << 20) % (margin + 1)
    lengths = lengths.at[giver].add(-passed).at[sink].add(passed)
    labels = jnp.searchsorted(jnp.cumsum(lengths), jnp.arange(rows * top), side="right").astype(jnp.int32)
    listing = labels.reshape(top, rows).T
    listing = listing[jax.random.permutation(jax.random.fold_in(own, 1), rows)]
    offset_by = jax.random.randint(jax.random.fold_in(own, 2), (rows, 1), 0, top)
    return jnp.take_along_axis(listing, (jnp.arange(top)[None, :] + offset_by) % top, axis=1)


def portions_of(count, total, bound, lean, full):
    weights = [(1 << 20) // math.isqrt(grade ** lean) + 1 for grade in range(1, count + 1)]
    largest = bound if full else min(bound, max(-(-total // count), total * weights[0] // sum(weights)))
    least = 1 if total - largest >= count - 1 else 0
    counts, spare = [largest] + [least] * (count - 1), total - largest - least * (count - 1)
    while spare > 0:
        candidates = [i for i in range(1, count) if counts[i] < largest] or [i for i in range(1, count) if counts[i] < bound]
        pool, left = sum([weights[i] for i in candidates]), spare
        for i in candidates:
            more = min(bound - counts[i], max(1, left * weights[i] // pool), spare)
            counts[i] = counts[i] + more
            spare = spare - more
    return np.array(counts)


def bell_draw(key, extent, spread, bound, cuts=(), kind=jnp.bfloat16):
    result = spread * jax.random.normal(key, extent, jnp.float32)
    if cuts:
        result = result * block_levels(key, extent, cuts, -0.22, 0.18)
    return jnp.clip(result, -bound, bound).astype(kind)


def setup_inputs(seed: int = 0) -> dict:
    arg_keys = jax.random.split(jax.random.key(seed), 8)
    tokens = bell_draw(arg_keys[0], (TOKENS, D), 1.0, 6.0, ((0, 4), (1, 8)))
    grad_out = bell_draw(arg_keys[1], (TOKENS, D), 1.0, 6.0, ((0, 4), (1, 8)))
    routes_keys = jax.random.split(jax.random.fold_in(arg_keys[2], 1), TOKENS // TOK_GRP)
    routes_turns = jax.random.permutation(jax.random.fold_in(arg_keys[2], 3), TOKENS // TOK_GRP)
    routes = jax.vmap(lambda own, number: routed_block(jax.random.fold_in(arg_keys[2], 2), own, number, TOK_GRP, EXPERTS, TOP, MOST, 2))(routes_keys, routes_turns).reshape((TOKENS, TOP))
    route_probs = jnp.clip(0.049804688 + 0.9501953 * jax.random.uniform(arg_keys[3], (TOKENS, TOP), jnp.float32) ** block_levels(arg_keys[3], (TOKENS, TOP), ((0, 4),), -0.2, 0.2), 0.049804688, 1.0).astype(jnp.bfloat16)
    gate_weight = bell_draw(arg_keys[4], (EXPERTS, D, UNITS), D ** -0.5, 0.0625, ((0, 4), (1, 8)))
    up_weight = bell_draw(arg_keys[5], (EXPERTS, D, UNITS), D ** -0.5, 0.0625, ((0, 4), (1, 8)))
    down_weight = bell_draw(arg_keys[6], (EXPERTS, UNITS, D), D ** -0.5, 0.0625, ((0, 4), (2, 8)))
    return {"tokens": tokens, "grad_out": grad_out, "routes": routes, "route_probs": route_probs, "gate_weight": gate_weight, "up_weight": up_weight, "down_weight": down_weight}


def silu_parts(gate):
    sig = jax.nn.sigmoid(gate)
    return gate * sig, sig * (1.0 + gate * (1.0 - sig))


def piece_sum(acts, weights):
    partial_prod = jnp.einsum("tlw,lwu->tlu", acts, weights)
    rounded = lax.optimization_barrier(partial_prod.astype(jnp.bfloat16))
    return jnp.sum(rounded.astype(jnp.float32), axis=1)


def reference(tokens, grad_out, routes, route_probs, gate_weight, up_weight, down_weight):
    width = D // N_LANE
    tok_wide = tokens.astype(jnp.float32).reshape(TOKENS, N_LANE, width)
    grad_wide = grad_out.astype(jnp.float32).reshape(TOKENS, N_LANE, width)
    probs_wide = route_probs.astype(jnp.float32)

    def expert(carry, index):
        token_acc, prob_acc = carry
        w_gate = gate_weight[index]
        w_up = up_weight[index]
        w_down = down_weight[index]
        gate = piece_sum(tok_wide, w_gate.astype(jnp.float32).reshape(N_LANE, width, UNITS))
        upward = piece_sum(tok_wide, w_up.astype(jnp.float32).reshape(N_LANE, width, UNITS))
        down_t = w_down.astype(jnp.float32).reshape(UNITS, N_LANE, width).transpose(1, 2, 0)
        grad = piece_sum(grad_wide, down_t)
        routed = routes == index
        weight = jnp.sum(jnp.where(routed, probs_wide, 0.0), axis=1)
        act, slope = silu_parts(gate)
        hidden = act * upward
        dprob = jnp.sum(hidden * grad, axis=1).astype(jnp.bfloat16)
        dhid = weight[:, None] * grad
        d_gate = (dhid * upward * slope).astype(jnp.bfloat16)
        d_up = (dhid * act).astype(jnp.bfloat16)
        scaled = (weight[:, None] * hidden).astype(jnp.bfloat16)
        contrib = jnp.dot(d_gate, w_gate.T, preferred_element_type=jnp.float32)
        contrib = contrib + jnp.dot(d_up, w_up.T, preferred_element_type=jnp.float32)
        contrib = lax.optimization_barrier(contrib.astype(jnp.bfloat16))
        token_acc = token_acc + contrib.astype(jnp.float32)
        prob_acc = jnp.where(routed, dprob[:, None], prob_acc)
        gate_g = jnp.dot(tokens.T, d_gate, preferred_element_type=jnp.float32).astype(jnp.bfloat16)
        up_g = jnp.dot(tokens.T, d_up, preferred_element_type=jnp.float32).astype(jnp.bfloat16)
        down_g = jnp.dot(scaled.T, grad_out, preferred_element_type=jnp.float32).astype(jnp.bfloat16)
        return (token_acc, prob_acc), (gate_g, up_g, down_g)

    start = (jnp.zeros((TOKENS, D), jnp.float32), jnp.zeros((TOKENS, TOP), jnp.bfloat16))
    (token_acc, prob_acc), (gate_grad, up_grad, down_grad) = lax.scan(expert, start, jnp.arange(EXPERTS))
    return token_acc.astype(jnp.bfloat16), prob_acc, gate_grad, up_grad, down_grad
```

```python
import functools

import jax
import jax.numpy as jnp
from jax import lax
from jax.experimental import pallas as pl
from jax.experimental.pallas import tpu as pltpu
from jax.sharding import PartitionSpec as P

MOST = 8
MESH = pl.DeviceIdType.MESH


def swiglu_back(gate, upward, grad, weight):
    sig = jax.nn.sigmoid(gate)
    act = gate * sig
    slope = sig * (1.0 + gate * (1.0 - sig))
    hidden = act * upward
    dprob = jnp.sum(hidden * grad, axis=1).astype(jnp.bfloat16)
    dhid = weight[:, None] * grad
    scaled = (weight[:, None] * hidden).astype(jnp.bfloat16)
    d_gate = (dhid * upward * slope).astype(jnp.bfloat16)
    d_up = (dhid * act).astype(jnp.bfloat16)
    return (scaled, d_gate, d_up, dprob)


def plain_shards(tokens, grad_out, routes, route_probs, gate_weight, up_weight, down_weight):
    groups = lax.axis_size("grp")
    lanes = lax.axis_size("lane")
    tok_rows, width = tokens.shape
    fanout = routes.shape[1]
    pairs = tok_rows * fanout
    expert_of = routes.reshape(pairs)
    onehot = (expert_of[:, None] == jnp.arange(groups, dtype=jnp.int32)[None, :]).astype(jnp.int32)
    before = jnp.cumsum(onehot, axis=0) - onehot
    slot_of = jnp.sum(before * onehot, axis=1)
    target = expert_of * MOST + slot_of
    row_count = groups * MOST
    placer = (jnp.arange(row_count, dtype=jnp.int32)[:, None] == target[None, :]).astype(
        jnp.bfloat16
    )
    tok_pairs = jnp.repeat(tokens, fanout, axis=0)
    grad_pairs = jnp.repeat(grad_out, fanout, axis=0)
    send_tok = jnp.dot(placer, tok_pairs, preferred_element_type=jnp.float32).astype(jnp.bfloat16)
    send_grad = jnp.dot(placer, grad_pairs, preferred_element_type=jnp.float32).astype(jnp.bfloat16)
    send_prob = jnp.dot(
        placer, route_probs.reshape(pairs, 1), preferred_element_type=jnp.float32
    ).astype(jnp.bfloat16)
    recv_tok, recv_grad, recv_prob = (
        lax.all_to_all(
            send_tok.reshape(groups, MOST, width), "grp", split_axis=0, concat_axis=0, tiled=True
        ),
        lax.all_to_all(
            send_grad.reshape(groups, MOST, width), "grp", split_axis=0, concat_axis=0, tiled=True
        ),
        lax.all_to_all(
            send_prob.reshape(groups, MOST), "grp", split_axis=0, concat_axis=0, tiled=True
        ),
    )
    rows_tok = recv_tok.reshape(row_count, width)
    rows_grad = recv_grad.reshape(row_count, width)
    rows_prob = recv_prob.reshape(row_count).astype(jnp.float32)
    w_gate = gate_weight[0]
    w_up = up_weight[0]
    w_down = down_weight[0]
    units = w_gate.shape[1]
    share = row_count // lanes
    gate_part = jnp.dot(rows_tok, w_gate, preferred_element_type=jnp.float32)
    up_part = jnp.dot(rows_tok, w_up, preferred_element_type=jnp.float32)
    grad_part = jnp.einsum("rd,ud->ru", rows_grad, w_down, preferred_element_type=jnp.float32)
    summed = lax.psum_scatter(
        jnp.concatenate((gate_part, up_part, grad_part), axis=1).astype(jnp.bfloat16),
        "lane",
        scatter_dimension=0,
        tiled=True,
    ).astype(jnp.float32)
    first = lax.axis_index("lane") * share
    mine = lax.dynamic_slice_in_dim(rows_prob, first, share, 0)
    part_scaled, part_gate, part_up, part_prob = swiglu_back(
        summed[:, :units], summed[:, units : 2 * units], summed[:, 2 * units :], mine
    )
    scaled, d_gate, d_up, dprob = (
        lax.all_gather(part_scaled, "lane", axis=0, tiled=True),
        lax.all_gather(part_gate, "lane", axis=0, tiled=True),
        lax.all_gather(part_up, "lane", axis=0, tiled=True),
        lax.all_gather(part_prob, "lane", axis=0, tiled=True),
    )
    contrib = jnp.einsum("ru,du->rd", d_gate, w_gate, preferred_element_type=jnp.float32)
    contrib = (
        contrib + jnp.einsum("ru,du->rd", d_up, w_up, preferred_element_type=jnp.float32)
    ).astype(jnp.bfloat16)
    gate_grad = jnp.einsum(
        "rd,ru->du", rows_tok, d_gate, preferred_element_type=jnp.float32
    ).astype(jnp.bfloat16)
    up_grad = jnp.einsum("rd,ru->du", rows_tok, d_up, preferred_element_type=jnp.float32).astype(
        jnp.bfloat16
    )
    down_grad = jnp.einsum(
        "ru,rd->ud", scaled, rows_grad, preferred_element_type=jnp.float32
    ).astype(jnp.bfloat16)
    back_tok, back_prob = (
        lax.all_to_all(
            contrib.reshape(groups, MOST, width), "grp", split_axis=0, concat_axis=0, tiled=True
        ),
        lax.all_to_all(dprob.reshape(groups, MOST), "grp", split_axis=0, concat_axis=0, tiled=True),
    )
    picked = jnp.dot(
        placer.T, back_tok.reshape(row_count, width), preferred_element_type=jnp.float32
    )
    token_grad = jnp.sum(picked.reshape(tok_rows, fanout, width), axis=1).astype(jnp.bfloat16)
    prob_grad = jnp.dot(
        placer.T, back_prob.reshape(row_count, 1), preferred_element_type=jnp.float32
    )
    prob_grad = prob_grad.astype(jnp.bfloat16).reshape(tok_rows, fanout)
    return (token_grad, prob_grad, gate_grad[None], up_grad[None], down_grad[None])


def tn_dot(a, b):
    return lax.dot_general(a, b, (((0,), (0,)), ((), ())), preferred_element_type=jnp.float32)


def nt_dot(a, b):
    return lax.dot_general(a, b, (((1,), (1,)), ((), ())), preferred_element_type=jnp.float32)


def fused(
    groups,
    lanes,
    tok_ref,
    cot_ref,
    routes_ref,
    probs_ref,
    wg_hbm,
    wu_hbm,
    wd_hbm,
    tg_ref,
    pg_ref,
    gg_hbm,
    ug_hbm,
    dg_hbm,
    wg,
    wu,
    wd,
    gg,
    ug,
    dg,
    send_a,
    recv_a,
    send_rs,
    recv_rs,
    gat,
    send_b,
    recv_b,
    win_sem,
    wout_sem,
    sa_sem,
    ra_sem,
    ss_sem,
    rs_sem,
    sg_sem,
    rg_sem,
    sb_sem,
    rb_sem,
):
    f32, bf16 = jnp.float32, jnp.bfloat16
    g_me = lax.axis_index("grp")
    l_me = lax.axis_index("lane")
    tok_rows, width = tok_ref.shape
    fanout = routes_ref.shape[1]
    units = wg.shape[1]
    chunk = units // lanes
    rows = groups * MOST
    left = send_b.shape[2]
    grp_peers = [lax.rem(g_me + j, groups) for j in range(1, groups)]
    lane_peers = [lax.rem(l_me + j, lanes) for j in range(1, lanes)]

    barrier = pltpu.get_barrier_semaphore()
    for g in grp_peers:
        pl.semaphore_signal(barrier, inc=1, device_id=(g, l_me), device_id_type=MESH)
    for l in lane_peers:
        pl.semaphore_signal(barrier, inc=1, device_id=(g_me, l), device_id_type=MESH)

    loads = [
        pltpu.make_async_copy(wg_hbm.at[0], wg, win_sem.at[0]),
        pltpu.make_async_copy(wu_hbm.at[0], wu, win_sem.at[1]),
        pltpu.make_async_copy(wd_hbm.at[0], wd, win_sem.at[2]),
    ]
    for load in loads:
        load.start()

    r_wide = routes_ref[...]
    p_wide = probs_ref[...].astype(f32)
    t_row = lax.broadcasted_iota(jnp.int32, (tok_rows, tok_rows), 0)
    t_col = lax.broadcasted_iota(jnp.int32, (tok_rows, tok_rows), 1)
    eye = t_row == t_col
    row_id = lax.broadcasted_iota(jnp.int32, (rows, tok_rows), 0)
    col_id = lax.broadcasted_iota(jnp.int32, (tok_rows, rows), 1)
    row_exp, row_slot = row_id // MOST, row_id % MOST
    col_exp, col_slot = col_id // MOST, col_id % MOST
    named = jnp.zeros((rows, tok_rows), f32)
    chance = jnp.zeros((rows, tok_rows), f32)
    named_t = jnp.zeros((tok_rows, rows), f32)
    hits = []
    for k in range(fanout):
        r_col = r_wide[:, k : k + 1].astype(f32)
        p_col = p_wide[:, k : k + 1]
        r_lane = jnp.sum(jnp.where(eye, r_col, 0.0), axis=0, keepdims=True)
        p_lane = jnp.sum(jnp.where(eye, p_col, 0.0), axis=0, keepdims=True)
        hit = (row_exp.astype(f32) == r_lane).astype(f32)
        named = named + hit
        chance = chance + hit * p_lane
        hit_t = (col_exp.astype(f32) == r_col).astype(f32)
        named_t = named_t + hit_t
        hits.append(hit_t)
    before = jnp.dot(
        named.astype(bf16), (t_row < t_col).astype(bf16), preferred_element_type=f32
    )
    before_t = jnp.dot(
        (t_col < t_row).astype(bf16), named_t.astype(bf16), preferred_element_type=f32
    )
    placer = jnp.where(before == row_slot.astype(f32), named, 0.0)
    placer_t = jnp.where(before_t == col_slot.astype(f32), named_t, 0.0)
    row_prob = jnp.sum(placer * chance, axis=1, keepdims=True)
    placed = placer.astype(bf16)
    out_tok = jnp.dot(placed, tok_ref[...], preferred_element_type=f32)
    out_cot = jnp.dot(placed, cot_ref[...], preferred_element_type=f32)
    prob_tile = jnp.broadcast_to(row_prob, (rows, chunk))
    for e in range(groups):
        at = slice(e * MOST, (e + 1) * MOST)
        send_a[e, :, :width] = jnp.concatenate((out_tok[at], out_cot[at]), axis=0).astype(bf16)
        send_a[e, :, width:] = jnp.concatenate((prob_tile[at], prob_tile[at]), axis=0).astype(bf16)

    pl.semaphore_wait(barrier, groups + lanes - 2)

    def a_copy(to, slot):
        return pltpu.make_async_remote_copy(
            src_ref=send_a.at[to],
            dst_ref=recv_a.at[slot],
            send_sem=sa_sem.at[to],
            recv_sem=ra_sem.at[slot],
            device_id=(to, l_me),
            device_id_type=MESH,
        )

    for g in grp_peers:
        a_copy(g, g_me).start()
    recv_a[g_me] = send_a[g_me]
    for load in loads:
        load.wait()
    for g in grp_peers:
        a_copy(g, g).wait_recv()

    tok_in, cot_in, prob_in = [], [], []
    for g in range(groups):
        both = recv_a[g].astype(f32)
        tok_in.append(both[:MOST, :width])
        cot_in.append(both[MOST:, :width])
        prob_in.append(both[:MOST, width:])
    rows_tok = jnp.concatenate(tok_in, axis=0).astype(bf16)
    rows_cot = jnp.concatenate(cot_in, axis=0).astype(bf16)
    prob = jnp.concatenate(prob_in, axis=0)

    def rs_copy(to, slot):
        return pltpu.make_async_remote_copy(
            src_ref=send_rs.at[to],
            dst_ref=recv_rs.at[slot],
            send_sem=ss_sem.at[to],
            recv_sem=rs_sem.at[slot],
            device_id=(g_me, to),
            device_id_type=MESH,
        )

    chips = lanes // 2
    chip_me, core_me = l_me // 2, l_me % 2
    for j in range(1, chips + 1):
        chip = lax.rem(chip_me + j, chips)
        at = pl.ds(pl.multiple_of(chip * (2 * chunk), 2 * chunk), 2 * chunk)
        parts = (
            jnp.dot(rows_tok, wg[:, at], preferred_element_type=f32).astype(bf16),
            jnp.dot(rows_tok, wu[:, at], preferred_element_type=f32).astype(bf16),
            nt_dot(rows_cot, wd[at, :]).astype(bf16),
        )
        for h in range(2):
            for i, part in enumerate(parts):
                send_rs[2 * chip + h, :, i * chunk : (i + 1) * chunk] = part[
                    :, h * chunk : (h + 1) * chunk
                ]
            if j < chips:
                rs_copy(2 * chip + h, l_me).start()
    rs_copy(2 * chip_me + 1 - core_me, l_me).start()
    recv_rs[l_me] = send_rs[l_me]
    for l in lane_peers:
        rs_copy(l, l).wait_recv()

    summed = recv_rs[0].astype(f32)
    for l in range(1, lanes):
        summed = summed + recv_rs[l].astype(f32)
    gate, upward, grad = (summed[:, i * chunk : (i + 1) * chunk] for i in range(3))
    sig = jax.nn.sigmoid(gate)
    act = gate * sig
    slope = sig * (1.0 + gate * (1.0 - sig))
    hidden = act * upward
    dpart = jnp.sum(hidden * grad, axis=1, keepdims=True)
    dhid = prob * grad
    gat[l_me, :, :chunk] = (dhid * upward * slope).astype(bf16)
    gat[l_me, :, chunk : 2 * chunk] = (dhid * act).astype(bf16)
    gat[l_me, :, 2 * chunk : 3 * chunk] = (prob * hidden).astype(bf16)
    high = dpart.astype(bf16).astype(f32)
    lane_id = lax.broadcasted_iota(jnp.int32, (rows, chunk), 1)
    gat[l_me, :, 3 * chunk :] = jnp.where(lane_id < chunk // 2, high, dpart - high).astype(bf16)

    def ag_copy(to, slot):
        return pltpu.make_async_remote_copy(
            src_ref=gat.at[slot],
            dst_ref=gat.at[slot],
            send_sem=sg_sem.at[to],
            recv_sem=rg_sem.at[slot],
            device_id=(g_me, to),
            device_id_type=MESH,
        )

    for l in lane_peers:
        ag_copy(l, l_me).start()
    for l in lane_peers:
        ag_copy(l, l).wait_recv()

    d_gate = jnp.concatenate([gat[l, :, :chunk] for l in range(lanes)], axis=1)
    d_up = jnp.concatenate([gat[l, :, chunk : 2 * chunk] for l in range(lanes)], axis=1)
    scaled = jnp.concatenate([gat[l, :, 2 * chunk : 3 * chunk] for l in range(lanes)], axis=1)
    dtile = gat[0, :, 3 * chunk :].astype(f32)
    for l in range(1, lanes):
        dtile = dtile + gat[l, :, 3 * chunk :].astype(f32)
    dprob = jnp.sum(dtile, axis=1, keepdims=True) * (2.0 / chunk)
    dprob = jnp.broadcast_to(dprob, (rows, 128))

    contrib = nt_dot(d_gate, wg[...]) + nt_dot(d_up, wu[...])
    for e in range(groups):
        at = slice(e * MOST, (e + 1) * MOST)
        right = jnp.concatenate((contrib[at, left:], dprob[at]), axis=1)
        pad = left - right.shape[1]
        if pad:
            right = jnp.concatenate((right, jnp.zeros((MOST, pad), f32)), axis=1)
        send_b[e] = jnp.concatenate((contrib[at, :left], right), axis=0).astype(bf16)

    def b_copy(to, slot):
        return pltpu.make_async_remote_copy(
            src_ref=send_b.at[to],
            dst_ref=recv_b.at[slot],
            send_sem=sb_sem.at[to],
            recv_sem=rb_sem.at[slot],
            device_id=(to, l_me),
            device_id_type=MESH,
        )

    for g in grp_peers:
        b_copy(g, g_me).start()
    recv_b[g_me] = send_b[g_me]

    stores = [
        pltpu.make_async_copy(gg, gg_hbm.at[0], wout_sem.at[0]),
        pltpu.make_async_copy(ug, ug_hbm.at[0], wout_sem.at[1]),
        pltpu.make_async_copy(dg, dg_hbm.at[0], wout_sem.at[2]),
    ]
    gg[...] = tn_dot(rows_tok, d_gate).astype(bf16)
    stores[0].start()
    ug[...] = tn_dot(rows_tok, d_up).astype(bf16)
    stores[1].start()
    dg[...] = tn_dot(scaled, rows_cot).astype(bf16)
    stores[2].start()

    for g in grp_peers:
        b_copy(g, g).wait_recv()
    low, top = [], []
    for g in range(groups):
        both = recv_b[g].astype(f32)
        low.append(both[:MOST])
        top.append(both[MOST:])
    low = jnp.concatenate(low, axis=0).astype(bf16)
    top = jnp.concatenate(top, axis=0).astype(bf16)
    back = placer_t.astype(bf16)
    tg_ref[:, :left] = jnp.dot(back, low, preferred_element_type=f32).astype(bf16)
    tg_ref[:, left:] = jnp.dot(
        back, top[:, : width - left], preferred_element_type=f32
    ).astype(bf16)
    dback = top[:, width - left : width - left + 128]
    pick = lax.broadcasted_iota(jnp.int32, (tok_rows, 128), 1)
    result = jnp.zeros((tok_rows, 128), f32)
    for k in range(fanout):
        mine = jnp.dot((placer_t * hits[k]).astype(bf16), dback, preferred_element_type=f32)
        result = jnp.where(pick == k, mine, result)
    pg_ref[...] = result[:, :fanout].astype(bf16)

    for g in grp_peers:
        a_copy(g, g_me).wait_send()
        b_copy(g, g_me).wait_send()
    for l in lane_peers:
        rs_copy(l, l_me).wait_send()
        ag_copy(l, l_me).wait_send()
    for store in stores:
        store.wait()


def shards(tokens, grad_out, routes, route_probs, gate_weight, up_weight, down_weight):
    groups = lax.axis_size("grp")
    lanes = lax.axis_size("lane")
    tok_rows, width = tokens.shape
    units = gate_weight.shape[2]
    chunk = units // lanes
    args = (tokens, grad_out, routes, route_probs, gate_weight, up_weight, down_weight)
    if width % 128 or chunk % 128 or lanes % 2 or tok_rows % 16:
        return plain_shards(*args)
    rows = groups * MOST
    left = 128 * ((width // 128 + 2) // 2)
    bf16 = jnp.bfloat16
    vmem = pl.BlockSpec(memory_space=pltpu.VMEM)
    hbm = pl.BlockSpec(memory_space=pl.ANY)
    dma = pltpu.SemaphoreType.DMA
    return pl.pallas_call(
        functools.partial(fused, groups, lanes),
        out_shape=(
            jax.ShapeDtypeStruct(tokens.shape, bf16),
            jax.ShapeDtypeStruct(route_probs.shape, bf16),
            jax.ShapeDtypeStruct(gate_weight.shape, bf16),
            jax.ShapeDtypeStruct(up_weight.shape, bf16),
            jax.ShapeDtypeStruct(down_weight.shape, bf16),
        ),
        in_specs=[vmem] * 4 + [hbm] * 3,
        out_specs=(vmem, vmem, hbm, hbm, hbm),
        scratch_shapes=[
            pltpu.VMEM((width, units), bf16),
            pltpu.VMEM((width, units), bf16),
            pltpu.VMEM((units, width), bf16),
            pltpu.VMEM((width, units), bf16),
            pltpu.VMEM((width, units), bf16),
            pltpu.VMEM((units, width), bf16),
            pltpu.VMEM((groups, 2 * MOST, width + chunk), bf16),
            pltpu.VMEM((groups, 2 * MOST, width + chunk), bf16),
            pltpu.VMEM((lanes, rows, 3 * chunk), bf16),
            pltpu.VMEM((lanes, rows, 3 * chunk), bf16),
            pltpu.VMEM((lanes, rows, 4 * chunk), bf16),
            pltpu.VMEM((groups, 2 * MOST, left), bf16),
            pltpu.VMEM((groups, 2 * MOST, left), bf16),
            dma((3,)),
            dma((3,)),
            dma((groups,)),
            dma((groups,)),
            dma((lanes,)),
            dma((lanes,)),
            dma((lanes,)),
            dma((lanes,)),
            dma((groups,)),
            dma((groups,)),
        ],
        compiler_params=pltpu.CompilerParams(
            collective_id=0, has_side_effects=True, vmem_limit_bytes=48 * 1024 * 1024
        ),
    )(*args)


def solution(mesh):
    placed = (
        P("grp", "lane"),
        P("grp", "lane"),
        P("grp", None),
        P("grp", None),
        P("grp", "lane", None),
        P("grp", "lane", None),
        P("grp", None, "lane"),
    )
    return jax.shard_map(
        shards,
        mesh=mesh,
        in_specs=placed,
        out_specs=(
            P("grp", "lane"),
            P("grp", None),
            P("grp", "lane", None),
            P("grp", "lane", None),
            P("grp", None, "lane"),
        ),
        check_vma=False,
    )
```

```python
import functools

import jax
import jax.numpy as jnp
from jax import lax
from jax.experimental import pallas as pl
from jax.experimental.pallas import tpu as pltpu
from jax.sharding import PartitionSpec as P

MOST = 8
MESH = pl.DeviceIdType.MESH


def swiglu_back(gate, upward, grad, weight):
    sig = jax.nn.sigmoid(gate)
    act = gate * sig
    slope = sig * (1.0 + gate * (1.0 - sig))
    hidden = act * upward
    dprob = jnp.sum(hidden * grad, axis=1).astype(jnp.bfloat16)
    dhid = weight[:, None] * grad
    scaled = (weight[:, None] * hidden).astype(jnp.bfloat16)
    d_gate = (dhid * upward * slope).astype(jnp.bfloat16)
    d_up = (dhid * act).astype(jnp.bfloat16)
    return (scaled, d_gate, d_up, dprob)


def plain_shards(tokens, grad_out, routes, route_probs, gate_weight, up_weight, down_weight):
    groups = lax.axis_size("grp")
    lanes = lax.axis_size("lane")
    tok_rows, width = tokens.shape
    fanout = routes.shape[1]
    pairs = tok_rows * fanout
    expert_of = routes.reshape(pairs)
    onehot = (expert_of[:, None] == jnp.arange(groups, dtype=jnp.int32)[None, :]).astype(jnp.int32)
    before = jnp.cumsum(onehot, axis=0) - onehot
    slot_of = jnp.sum(before * onehot, axis=1)
    target = expert_of * MOST + slot_of
    row_count = groups * MOST
    placer = (jnp.arange(row_count, dtype=jnp.int32)[:, None] == target[None, :]).astype(
        jnp.bfloat16
    )
    tok_pairs = jnp.repeat(tokens, fanout, axis=0)
    grad_pairs = jnp.repeat(grad_out, fanout, axis=0)
    send_tok = jnp.dot(placer, tok_pairs, preferred_element_type=jnp.float32).astype(jnp.bfloat16)
    send_grad = jnp.dot(placer, grad_pairs, preferred_element_type=jnp.float32).astype(jnp.bfloat16)
    send_prob = jnp.dot(
        placer, route_probs.reshape(pairs, 1), preferred_element_type=jnp.float32
    ).astype(jnp.bfloat16)
    recv_tok, recv_grad, recv_prob = (
        lax.all_to_all(
            send_tok.reshape(groups, MOST, width), "grp", split_axis=0, concat_axis=0, tiled=True
        ),
        lax.all_to_all(
            send_grad.reshape(groups, MOST, width), "grp", split_axis=0, concat_axis=0, tiled=True
        ),
        lax.all_to_all(
            send_prob.reshape(groups, MOST), "grp", split_axis=0, concat_axis=0, tiled=True
        ),
    )
    rows_tok = recv_tok.reshape(row_count, width)
    rows_grad = recv_grad.reshape(row_count, width)
    rows_prob = recv_prob.reshape(row_count).astype(jnp.float32)
    w_gate = gate_weight[0]
    w_up = up_weight[0]
    w_down = down_weight[0]
    units = w_gate.shape[1]
    share = row_count // lanes
    gate_part = jnp.dot(rows_tok, w_gate, preferred_element_type=jnp.float32)
    up_part = jnp.dot(rows_tok, w_up, preferred_element_type=jnp.float32)
    grad_part = jnp.einsum("rd,ud->ru", rows_grad, w_down, preferred_element_type=jnp.float32)
    summed = lax.psum_scatter(
        jnp.concatenate((gate_part, up_part, grad_part), axis=1).astype(jnp.bfloat16),
        "lane",
        scatter_dimension=0,
        tiled=True,
    ).astype(jnp.float32)
    first = lax.axis_index("lane") * share
    mine = lax.dynamic_slice_in_dim(rows_prob, first, share, 0)
    part_scaled, part_gate, part_up, part_prob = swiglu_back(
        summed[:, :units], summed[:, units : 2 * units], summed[:, 2 * units :], mine
    )
    scaled, d_gate, d_up, dprob = (
        lax.all_gather(part_scaled, "lane", axis=0, tiled=True),
        lax.all_gather(part_gate, "lane", axis=0, tiled=True),
        lax.all_gather(part_up, "lane", axis=0, tiled=True),
        lax.all_gather(part_prob, "lane", axis=0, tiled=True),
    )
    contrib = jnp.einsum("ru,du->rd", d_gate, w_gate, preferred_element_type=jnp.float32)
    contrib = (
        contrib + jnp.einsum("ru,du->rd", d_up, w_up, preferred_element_type=jnp.float32)
    ).astype(jnp.bfloat16)
    gate_grad = jnp.einsum(
        "rd,ru->du", rows_tok, d_gate, preferred_element_type=jnp.float32
    ).astype(jnp.bfloat16)
    up_grad = jnp.einsum("rd,ru->du", rows_tok, d_up, preferred_element_type=jnp.float32).astype(
        jnp.bfloat16
    )
    down_grad = jnp.einsum(
        "ru,rd->ud", scaled, rows_grad, preferred_element_type=jnp.float32
    ).astype(jnp.bfloat16)
    back_tok, back_prob = (
        lax.all_to_all(
            contrib.reshape(groups, MOST, width), "grp", split_axis=0, concat_axis=0, tiled=True
        ),
        lax.all_to_all(dprob.reshape(groups, MOST), "grp", split_axis=0, concat_axis=0, tiled=True),
    )
    picked = jnp.dot(
        placer.T, back_tok.reshape(row_count, width), preferred_element_type=jnp.float32
    )
    token_grad = jnp.sum(picked.reshape(tok_rows, fanout, width), axis=1).astype(jnp.bfloat16)
    prob_grad = jnp.dot(
        placer.T, back_prob.reshape(row_count, 1), preferred_element_type=jnp.float32
    )
    prob_grad = prob_grad.astype(jnp.bfloat16).reshape(tok_rows, fanout)
    return (token_grad, prob_grad, gate_grad[None], up_grad[None], down_grad[None])


def nt_dot(a, b):
    return lax.dot_general(a, b, (((1,), (1,)), ((), ())), preferred_element_type=jnp.float32)


def fused(
    groups,
    lanes,
    routes_ref,
    probs_ref,
    tok_hbm,
    cot_hbm,
    wg_hbm,
    wu_hbm,
    wd_hbm,
    tg_ref,
    pg_ref,
    tok_t_ref,
    sc_t_ref,
    cot_rows_ref,
    d_gate_ref,
    d_up_ref,
    tok_ref,
    cot_ref,
    wg,
    wu,
    wd,
    send_a,
    recv_a,
    send_rs,
    recv_rs,
    gat,
    send_b,
    recv_b,
    win_sem,
    sa_sem,
    ra_sem,
    ss_sem,
    rs_sem,
    sg_sem,
    rg_sem,
    sb_sem,
    rb_sem,
):
    f32, bf16 = jnp.float32, jnp.bfloat16
    g_me = lax.axis_index("grp")
    l_me = lax.axis_index("lane")
    tok_rows, width = tok_ref.shape
    fanout = routes_ref.shape[0]
    units = wg.shape[1]
    chunk = units // lanes
    rows = groups * MOST
    left = send_b.shape[2]
    grp_peers = [lax.rem(g_me + j, groups) for j in range(1, groups)]
    lane_peers = [lax.rem(l_me + j, lanes) for j in range(1, lanes)]

    barrier = pltpu.get_barrier_semaphore()
    for g in grp_peers:
        pl.semaphore_signal(barrier, inc=1, device_id=(g, l_me), device_id_type=MESH)
    for l in lane_peers:
        pl.semaphore_signal(barrier, inc=1, device_id=(g_me, l), device_id_type=MESH)

    first = [
        pltpu.make_async_copy(tok_hbm, tok_ref, win_sem.at[3]),
        pltpu.make_async_copy(cot_hbm, cot_ref, win_sem.at[4]),
    ]
    loads = [
        pltpu.make_async_copy(wg_hbm.at[0], wg, win_sem.at[0]),
        pltpu.make_async_copy(wu_hbm.at[0], wu, win_sem.at[1]),
        pltpu.make_async_copy(wd_hbm.at[0], wd, win_sem.at[2]),
    ]
    for load in first + loads:
        load.start()

    r_wide = routes_ref[...]
    p_wide = probs_ref[...].astype(f32)
    t_row = lax.broadcasted_iota(jnp.int32, (tok_rows, tok_rows), 0)
    t_col = lax.broadcasted_iota(jnp.int32, (tok_rows, tok_rows), 1)
    eye = t_row == t_col
    row_id = lax.broadcasted_iota(jnp.int32, (rows, tok_rows), 0)
    col_id = lax.broadcasted_iota(jnp.int32, (tok_rows, rows), 1)
    row_exp, row_slot = row_id // MOST, row_id % MOST
    col_exp, col_slot = col_id // MOST, col_id % MOST
    named = jnp.zeros((rows, tok_rows), f32)
    chance = jnp.zeros((rows, tok_rows), f32)
    named_t = jnp.zeros((tok_rows, rows), f32)
    hits = []
    for k in range(fanout):
        r_lane = r_wide[k : k + 1].astype(f32)
        p_lane = p_wide[k : k + 1]
        r_col = jnp.sum(jnp.where(eye, r_lane, 0.0), axis=1, keepdims=True)
        hit = (row_exp.astype(f32) == r_lane).astype(f32)
        named = named + hit
        chance = chance + hit * p_lane
        hit_t = (col_exp.astype(f32) == r_col).astype(f32)
        named_t = named_t + hit_t
        hits.append(hit_t)
    before = jnp.dot(
        named.astype(bf16), (t_row < t_col).astype(bf16), preferred_element_type=f32
    )
    before_t = jnp.dot(
        (t_col < t_row).astype(bf16), named_t.astype(bf16), preferred_element_type=f32
    )
    placer = jnp.where(before == row_slot.astype(f32), named, 0.0)
    placer_t = jnp.where(before_t == col_slot.astype(f32), named_t, 0.0)
    row_prob = jnp.sum(placer * chance, axis=1, keepdims=True)
    placed = placer.astype(bf16)
    for load in first:
        load.wait()
    out_tok = jnp.dot(placed, tok_ref[...], preferred_element_type=f32)
    out_cot = jnp.dot(placed, cot_ref[...], preferred_element_type=f32)
    prob_tile = jnp.broadcast_to(row_prob, (rows, chunk))
    for e in range(groups):
        at = slice(e * MOST, (e + 1) * MOST)
        send_a[e, :, :width] = jnp.concatenate((out_tok[at], out_cot[at]), axis=0).astype(bf16)
        send_a[e, :, width:] = jnp.concatenate((prob_tile[at], prob_tile[at]), axis=0).astype(bf16)

    pl.semaphore_wait(barrier, groups + lanes - 2)

    def a_copy(to, slot):
        return pltpu.make_async_remote_copy(
            src_ref=send_a.at[to],
            dst_ref=recv_a.at[slot],
            send_sem=sa_sem.at[to],
            recv_sem=ra_sem.at[slot],
            device_id=(to, l_me),
            device_id_type=MESH,
        )

    for g in grp_peers:
        a_copy(g, g_me).start()
    recv_a[g_me] = send_a[g_me]
    for load in loads:
        load.wait()
    for g in grp_peers:
        a_copy(g, g).wait_recv()

    tok_in, cot_in, prob_in = [], [], []
    for g in range(groups):
        both = recv_a[g].astype(f32)
        tok_in.append(both[:MOST, :width])
        cot_in.append(both[MOST:, :width])
        prob_in.append(both[:MOST, width:])
    rows_tok = jnp.concatenate(tok_in, axis=0).astype(bf16)
    rows_cot = jnp.concatenate(cot_in, axis=0).astype(bf16)
    prob = jnp.concatenate(prob_in, axis=0)

    def rs_copy(to, slot):
        return pltpu.make_async_remote_copy(
            src_ref=send_rs.at[to],
            dst_ref=recv_rs.at[slot],
            send_sem=ss_sem.at[to],
            recv_sem=rs_sem.at[slot],
            device_id=(g_me, to),
            device_id_type=MESH,
        )

    chips = lanes // 2
    chip_me, core_me = l_me // 2, l_me % 2
    for j in range(1, chips + 1):
        chip = lax.rem(chip_me + j, chips)
        at = pl.ds(pl.multiple_of(chip * (2 * chunk), 2 * chunk), 2 * chunk)
        parts = (
            jnp.dot(rows_tok, wg[:, at], preferred_element_type=f32).astype(bf16),
            jnp.dot(rows_tok, wu[:, at], preferred_element_type=f32).astype(bf16),
            nt_dot(rows_cot, wd[at, :]).astype(bf16),
        )
        for h in range(2):
            for i, part in enumerate(parts):
                send_rs[2 * chip + h, :, i * chunk : (i + 1) * chunk] = part[
                    :, h * chunk : (h + 1) * chunk
                ]
            if j < chips:
                rs_copy(2 * chip + h, l_me).start()
    rs_copy(2 * chip_me + 1 - core_me, l_me).start()
    recv_rs[l_me] = send_rs[l_me]
    for l in lane_peers:
        rs_copy(l, l).wait_recv()

    summed = recv_rs[0].astype(f32)
    for l in range(1, lanes):
        summed = summed + recv_rs[l].astype(f32)
    gate, upward, grad = (summed[:, i * chunk : (i + 1) * chunk] for i in range(3))
    sig = jax.nn.sigmoid(gate)
    act = gate * sig
    slope = sig * (1.0 + gate * (1.0 - sig))
    hidden = act * upward
    dpart = jnp.sum(hidden * grad, axis=1, keepdims=True)
    dhid = prob * grad
    gat[l_me, :, :chunk] = (dhid * upward * slope).astype(bf16)
    gat[l_me, :, chunk : 2 * chunk] = (dhid * act).astype(bf16)
    gat[l_me, :, 2 * chunk : 3 * chunk] = (prob * hidden).astype(bf16)
    high = dpart.astype(bf16).astype(f32)
    lane_id = lax.broadcasted_iota(jnp.int32, (rows, chunk), 1)
    gat[l_me, :, 3 * chunk :] = jnp.where(lane_id < chunk // 2, high, dpart - high).astype(bf16)

    def ag_copy(to, slot):
        return pltpu.make_async_remote_copy(
            src_ref=gat.at[slot],
            dst_ref=gat.at[slot],
            send_sem=sg_sem.at[to],
            recv_sem=rg_sem.at[slot],
            device_id=(g_me, to),
            device_id_type=MESH,
        )

    for l in lane_peers:
        ag_copy(l, l_me).start()
    for l in lane_peers:
        ag_copy(l, l).wait_recv()

    d_gate = jnp.concatenate([gat[l, :, :chunk] for l in range(lanes)], axis=1)
    d_up = jnp.concatenate([gat[l, :, chunk : 2 * chunk] for l in range(lanes)], axis=1)
    scaled = jnp.concatenate([gat[l, :, 2 * chunk : 3 * chunk] for l in range(lanes)], axis=1)
    dtile = gat[0, :, 3 * chunk :].astype(f32)
    for l in range(1, lanes):
        dtile = dtile + gat[l, :, 3 * chunk :].astype(f32)
    dprob = jnp.sum(dtile, axis=1, keepdims=True) * (2.0 / chunk)
    dprob = jnp.broadcast_to(dprob, (rows, 128))

    contrib = nt_dot(d_gate, wg[...]) + nt_dot(d_up, wu[...])
    for e in range(groups):
        at = slice(e * MOST, (e + 1) * MOST)
        right = jnp.concatenate((contrib[at, left:], dprob[at]), axis=1)
        pad = left - right.shape[1]
        if pad:
            right = jnp.concatenate((right, jnp.zeros((MOST, pad), f32)), axis=1)
        send_b[e] = jnp.concatenate((contrib[at, :left], right), axis=0).astype(bf16)

    def b_copy(to, slot):
        return pltpu.make_async_remote_copy(
            src_ref=send_b.at[to],
            dst_ref=recv_b.at[slot],
            send_sem=sb_sem.at[to],
            recv_sem=rb_sem.at[slot],
            device_id=(to, l_me),
            device_id_type=MESH,
        )

    for g in grp_peers:
        b_copy(g, g_me).start()
    recv_b[g_me] = send_b[g_me]

    tok_t_ref[...] = rows_tok.astype(f32).T.astype(bf16)
    sc_t_ref[...] = scaled.astype(f32).T.astype(bf16)
    cot_rows_ref[...] = rows_cot
    d_gate_ref[...] = d_gate
    d_up_ref[...] = d_up

    for g in grp_peers:
        b_copy(g, g).wait_recv()
    low, top = [], []
    for g in range(groups):
        both = recv_b[g].astype(f32)
        low.append(both[:MOST])
        top.append(both[MOST:])
    low = jnp.concatenate(low, axis=0).astype(bf16)
    top = jnp.concatenate(top, axis=0).astype(bf16)
    back = placer_t.astype(bf16)
    tg_ref[:, :left] = jnp.dot(back, low, preferred_element_type=f32).astype(bf16)
    tg_ref[:, left:] = jnp.dot(
        back, top[:, : width - left], preferred_element_type=f32
    ).astype(bf16)
    dback = top[:, width - left : width - left + 128]
    for k in range(fanout):
        mine = jnp.dot((placer_t * hits[k]).astype(bf16), dback, preferred_element_type=f32)
        lane_row = jnp.sum(jnp.where(eye, mine[:, :1], 0.0), axis=0, keepdims=True)
        pg_ref[k : k + 1, :] = lane_row

    for g in grp_peers:
        a_copy(g, g_me).wait_send()
        b_copy(g, g_me).wait_send()
    for l in lane_peers:
        rs_copy(l, l_me).wait_send()
        ag_copy(l, l_me).wait_send()


def outer(tg_in, pg_in, tok_t, sc_t, cot_rows, d_gate, d_up, tg, pg, gg, ug, dg):
    f32, bf16 = jnp.float32, jnp.bfloat16

    @pl.when(pl.program_id(0) == 0)
    def _():
        tg[...] = tg_in[...]
        pg[...] = pg_in[...].astype(bf16)

    gg[0] = jnp.dot(tok_t[...], d_gate[...], preferred_element_type=f32).astype(bf16)
    ug[0] = jnp.dot(tok_t[...], d_up[...], preferred_element_type=f32).astype(bf16)
    dg[0] = jnp.dot(sc_t[...], cot_rows[...], preferred_element_type=f32).astype(bf16)


def shards(tokens, grad_out, routes, route_probs, gate_weight, up_weight, down_weight):
    groups = lax.axis_size("grp")
    lanes = lax.axis_size("lane")
    tok_rows, width = tokens.shape
    units = gate_weight.shape[2]
    chunk = units // lanes
    args = (tokens, grad_out, routes, route_probs, gate_weight, up_weight, down_weight)
    if width % 128 or chunk % 128 or lanes % 2 or tok_rows % 16:
        return plain_shards(*args)
    rows = groups * MOST
    left = 128 * ((width // 128 + 2) // 2)
    bf16 = jnp.bfloat16
    vmem = pl.BlockSpec(memory_space=pltpu.VMEM)
    hbm = pl.BlockSpec(memory_space=pltpu.HBM)
    dma = pltpu.SemaphoreType.DMA
    fanout = routes.shape[1]
    token_grad, prob_grad, tok_t, sc_t, cot_rows, d_gate, d_up = pl.pallas_call(
        functools.partial(fused, groups, lanes),
        out_shape=(
            jax.ShapeDtypeStruct(tokens.shape, bf16),
            jax.ShapeDtypeStruct((fanout, tok_rows), jnp.float32),
            jax.ShapeDtypeStruct((width, rows), bf16),
            jax.ShapeDtypeStruct((units, rows), bf16),
            jax.ShapeDtypeStruct((rows, width), bf16),
            jax.ShapeDtypeStruct((rows, units), bf16),
            jax.ShapeDtypeStruct((rows, units), bf16),
        ),
        in_specs=[vmem] * 2 + [hbm] * 5,
        out_specs=(vmem,) * 7,
        scratch_shapes=[
            pltpu.VMEM((tok_rows, width), bf16),
            pltpu.VMEM((tok_rows, width), bf16),
            pltpu.VMEM((width, units), bf16),
            pltpu.VMEM((width, units), bf16),
            pltpu.VMEM((units, width), bf16),
            pltpu.VMEM((groups, 2 * MOST, width + chunk), bf16),
            pltpu.VMEM((groups, 2 * MOST, width + chunk), bf16),
            pltpu.VMEM((lanes, rows, 3 * chunk), bf16),
            pltpu.VMEM((lanes, rows, 3 * chunk), bf16),
            pltpu.VMEM((lanes, rows, 4 * chunk), bf16),
            pltpu.VMEM((groups, 2 * MOST, left), bf16),
            pltpu.VMEM((groups, 2 * MOST, left), bf16),
            dma((5,)),
            dma((groups,)),
            dma((groups,)),
            dma((lanes,)),
            dma((lanes,)),
            dma((lanes,)),
            dma((lanes,)),
            dma((groups,)),
            dma((groups,)),
        ],
        compiler_params=pltpu.CompilerParams(
            collective_id=0, has_side_effects=True, vmem_limit_bytes=58 * 1024 * 1024
        ),
    )(routes.T, route_probs.T, tokens, grad_out, gate_weight, up_weight, down_weight)
    steps = 4
    wide, tall = units // steps, units // steps
    whole = lambda *shape: pl.BlockSpec(shape, lambda i: (0,) * len(shape))
    token_grad, prob_grad, gate_grad, up_grad, down_grad = pl.pallas_call(
        outer,
        grid=(steps,),
        out_shape=(
            jax.ShapeDtypeStruct(tokens.shape, bf16),
            jax.ShapeDtypeStruct((fanout, tok_rows), bf16),
            jax.ShapeDtypeStruct(gate_weight.shape, bf16),
            jax.ShapeDtypeStruct(up_weight.shape, bf16),
            jax.ShapeDtypeStruct(down_weight.shape, bf16),
        ),
        in_specs=[
            whole(tok_rows, width),
            whole(fanout, tok_rows),
            whole(width, rows),
            pl.BlockSpec((tall, rows), lambda i: (i, 0)),
            whole(rows, width),
            pl.BlockSpec((rows, wide), lambda i: (0, i)),
            pl.BlockSpec((rows, wide), lambda i: (0, i)),
        ],
        out_specs=(
            whole(tok_rows, width),
            whole(fanout, tok_rows),
            pl.BlockSpec((1, width, wide), lambda i: (0, 0, i)),
            pl.BlockSpec((1, width, wide), lambda i: (0, 0, i)),
            pl.BlockSpec((1, tall, width), lambda i: (0, i, 0)),
        ),
        compiler_params=pltpu.CompilerParams(vmem_limit_bytes=58 * 1024 * 1024),
    )(token_grad, prob_grad, tok_t, sc_t, cot_rows, d_gate, d_up)
    return token_grad, prob_grad.T, gate_grad, up_grad, down_grad


def solution(mesh):
    placed = (
        P("grp", "lane"),
        P("grp", "lane"),
        P("grp", None),
        P("grp", None),
        P("grp", "lane", None),
        P("grp", "lane", None),
        P("grp", None, "lane"),
    )
    return jax.shard_map(
        shards,
        mesh=mesh,
        in_specs=placed,
        out_specs=(
            P("grp", "lane"),
            P("grp", None),
            P("grp", "lane", None),
            P("grp", "lane", None),
            P("grp", None, "lane"),
        ),
        check_vma=False,
    )
```

```python
import functools

import jax
import jax.numpy as jnp
from jax import lax
from jax.experimental import pallas as pl
from jax.experimental.pallas import tpu as pltpu
from jax.sharding import PartitionSpec as P

MOST = 8
MESH = pl.DeviceIdType.MESH


def swiglu_back(gate, upward, grad, weight):
    sig = jax.nn.sigmoid(gate)
    act = gate * sig
    slope = sig * (1.0 + gate * (1.0 - sig))
    hidden = act * upward
    dprob = jnp.sum(hidden * grad, axis=1).astype(jnp.bfloat16)
    dhid = weight[:, None] * grad
    scaled = (weight[:, None] * hidden).astype(jnp.bfloat16)
    d_gate = (dhid * upward * slope).astype(jnp.bfloat16)
    d_up = (dhid * act).astype(jnp.bfloat16)
    return (scaled, d_gate, d_up, dprob)


def plain_shards(tokens, grad_out, routes, route_probs, gate_weight, up_weight, down_weight):
    groups = lax.axis_size("grp")
    lanes = lax.axis_size("lane")
    tok_rows, width = tokens.shape
    fanout = routes.shape[1]
    pairs = tok_rows * fanout
    expert_of = routes.reshape(pairs)
    onehot = (expert_of[:, None] == jnp.arange(groups, dtype=jnp.int32)[None, :]).astype(jnp.int32)
    before = jnp.cumsum(onehot, axis=0) - onehot
    slot_of = jnp.sum(before * onehot, axis=1)
    target = expert_of * MOST + slot_of
    row_count = groups * MOST
    placer = (jnp.arange(row_count, dtype=jnp.int32)[:, None] == target[None, :]).astype(
        jnp.bfloat16
    )
    tok_pairs = jnp.repeat(tokens, fanout, axis=0)
    grad_pairs = jnp.repeat(grad_out, fanout, axis=0)
    send_tok = jnp.dot(placer, tok_pairs, preferred_element_type=jnp.float32).astype(jnp.bfloat16)
    send_grad = jnp.dot(placer, grad_pairs, preferred_element_type=jnp.float32).astype(jnp.bfloat16)
    send_prob = jnp.dot(
        placer, route_probs.reshape(pairs, 1), preferred_element_type=jnp.float32
    ).astype(jnp.bfloat16)
    recv_tok, recv_grad, recv_prob = (
        lax.all_to_all(
            send_tok.reshape(groups, MOST, width), "grp", split_axis=0, concat_axis=0, tiled=True
        ),
        lax.all_to_all(
            send_grad.reshape(groups, MOST, width), "grp", split_axis=0, concat_axis=0, tiled=True
        ),
        lax.all_to_all(
            send_prob.reshape(groups, MOST), "grp", split_axis=0, concat_axis=0, tiled=True
        ),
    )
    rows_tok = recv_tok.reshape(row_count, width)
    rows_grad = recv_grad.reshape(row_count, width)
    rows_prob = recv_prob.reshape(row_count).astype(jnp.float32)
    w_gate = gate_weight[0]
    w_up = up_weight[0]
    w_down = down_weight[0]
    units = w_gate.shape[1]
    share = row_count // lanes
    gate_part = jnp.dot(rows_tok, w_gate, preferred_element_type=jnp.float32)
    up_part = jnp.dot(rows_tok, w_up, preferred_element_type=jnp.float32)
    grad_part = jnp.einsum("rd,ud->ru", rows_grad, w_down, preferred_element_type=jnp.float32)
    summed = lax.psum_scatter(
        jnp.concatenate((gate_part, up_part, grad_part), axis=1).astype(jnp.bfloat16),
        "lane",
        scatter_dimension=0,
        tiled=True,
    ).astype(jnp.float32)
    first = lax.axis_index("lane") * share
    mine = lax.dynamic_slice_in_dim(rows_prob, first, share, 0)
    part_scaled, part_gate, part_up, part_prob = swiglu_back(
        summed[:, :units], summed[:, units : 2 * units], summed[:, 2 * units :], mine
    )
    scaled, d_gate, d_up, dprob = (
        lax.all_gather(part_scaled, "lane", axis=0, tiled=True),
        lax.all_gather(part_gate, "lane", axis=0, tiled=True),
        lax.all_gather(part_up, "lane", axis=0, tiled=True),
        lax.all_gather(part_prob, "lane", axis=0, tiled=True),
    )
    contrib = jnp.einsum("ru,du->rd", d_gate, w_gate, preferred_element_type=jnp.float32)
    contrib = (
        contrib + jnp.einsum("ru,du->rd", d_up, w_up, preferred_element_type=jnp.float32)
    ).astype(jnp.bfloat16)
    gate_grad = jnp.einsum(
        "rd,ru->du", rows_tok, d_gate, preferred_element_type=jnp.float32
    ).astype(jnp.bfloat16)
    up_grad = jnp.einsum("rd,ru->du", rows_tok, d_up, preferred_element_type=jnp.float32).astype(
        jnp.bfloat16
    )
    down_grad = jnp.einsum(
        "ru,rd->ud", scaled, rows_grad, preferred_element_type=jnp.float32
    ).astype(jnp.bfloat16)
    back_tok, back_prob = (
        lax.all_to_all(
            contrib.reshape(groups, MOST, width), "grp", split_axis=0, concat_axis=0, tiled=True
        ),
        lax.all_to_all(dprob.reshape(groups, MOST), "grp", split_axis=0, concat_axis=0, tiled=True),
    )
    picked = jnp.dot(
        placer.T, back_tok.reshape(row_count, width), preferred_element_type=jnp.float32
    )
    token_grad = jnp.sum(picked.reshape(tok_rows, fanout, width), axis=1).astype(jnp.bfloat16)
    prob_grad = jnp.dot(
        placer.T, back_prob.reshape(row_count, 1), preferred_element_type=jnp.float32
    )
    prob_grad = prob_grad.astype(jnp.bfloat16).reshape(tok_rows, fanout)
    return (token_grad, prob_grad, gate_grad[None], up_grad[None], down_grad[None])


def nt_dot(a, b):
    return lax.dot_general(a, b, (((1,), (1,)), ((), ())), preferred_element_type=jnp.float32)


def fused(
    groups,
    lanes,
    routes_ref,
    probs_ref,
    tok_hbm,
    cot_hbm,
    wg_hbm,
    wu_hbm,
    wd_hbm,
    tg_ref,
    pg_ref,
    tok_t_ref,
    sc_t_ref,
    cot_rows_ref,
    d_gate_ref,
    d_up_ref,
    tok_ref,
    cot_ref,
    wg,
    wu,
    wd,
    send_a,
    recv_a,
    send_rs,
    recv_rs,
    gat,
    late,
    send_b,
    recv_b,
    win_sem,
    sa_sem,
    ra_sem,
    ss_sem,
    rs_sem,
    sg_sem,
    rg_sem,
    sl_sem,
    rl_sem,
    sb_sem,
    rb_sem,
):
    f32, bf16 = jnp.float32, jnp.bfloat16
    g_me = lax.axis_index("grp")
    l_me = lax.axis_index("lane")
    tok_rows, width = tok_ref.shape
    fanout = routes_ref.shape[0]
    units = wg.shape[1]
    chunk = units // lanes
    rows = groups * MOST
    left = send_b.shape[2]
    grp_peers = [lax.rem(g_me + j, groups) for j in range(1, groups)]
    lane_peers = [lax.rem(l_me + j, lanes) for j in range(1, lanes)]

    barrier = pltpu.get_barrier_semaphore()
    for g in grp_peers:
        pl.semaphore_signal(barrier, inc=1, device_id=(g, l_me), device_id_type=MESH)
    for l in lane_peers:
        pl.semaphore_signal(barrier, inc=1, device_id=(g_me, l), device_id_type=MESH)

    first = [
        pltpu.make_async_copy(tok_hbm, tok_ref, win_sem.at[3]),
        pltpu.make_async_copy(cot_hbm, cot_ref, win_sem.at[4]),
    ]
    loads = [
        pltpu.make_async_copy(wg_hbm.at[0], wg, win_sem.at[0]),
        pltpu.make_async_copy(wu_hbm.at[0], wu, win_sem.at[1]),
        pltpu.make_async_copy(wd_hbm.at[0], wd, win_sem.at[2]),
    ]
    for load in first + loads:
        load.start()

    r_wide = routes_ref[...]
    p_wide = probs_ref[...].astype(f32)
    t_row = lax.broadcasted_iota(jnp.int32, (tok_rows, tok_rows), 0)
    t_col = lax.broadcasted_iota(jnp.int32, (tok_rows, tok_rows), 1)
    eye = t_row == t_col
    row_id = lax.broadcasted_iota(jnp.int32, (rows, tok_rows), 0)
    col_id = lax.broadcasted_iota(jnp.int32, (tok_rows, rows), 1)
    row_exp, row_slot = row_id // MOST, row_id % MOST
    col_exp, col_slot = col_id // MOST, col_id % MOST
    named = jnp.zeros((rows, tok_rows), f32)
    chance = jnp.zeros((rows, tok_rows), f32)
    named_t = jnp.zeros((tok_rows, rows), f32)
    hits = []
    for k in range(fanout):
        r_lane = r_wide[k : k + 1].astype(f32)
        p_lane = p_wide[k : k + 1]
        r_col = jnp.sum(jnp.where(eye, r_lane, 0.0), axis=1, keepdims=True)
        hit = (row_exp.astype(f32) == r_lane).astype(f32)
        named = named + hit
        chance = chance + hit * p_lane
        hit_t = (col_exp.astype(f32) == r_col).astype(f32)
        named_t = named_t + hit_t
        hits.append(hit_t)
    before = jnp.dot(
        named.astype(bf16), (t_row < t_col).astype(bf16), preferred_element_type=f32
    )
    before_t = jnp.dot(
        (t_col < t_row).astype(bf16), named_t.astype(bf16), preferred_element_type=f32
    )
    placer = jnp.where(before == row_slot.astype(f32), named, 0.0)
    placer_t = jnp.where(before_t == col_slot.astype(f32), named_t, 0.0)
    row_prob = jnp.sum(placer * chance, axis=1, keepdims=True)
    placed = placer.astype(bf16)
    for load in first:
        load.wait()
    out_tok = jnp.dot(placed, tok_ref[...], preferred_element_type=f32)
    out_cot = jnp.dot(placed, cot_ref[...], preferred_element_type=f32)
    prob_tile = jnp.broadcast_to(row_prob, (rows, chunk))
    for e in range(groups):
        at = slice(e * MOST, (e + 1) * MOST)
        send_a[e, :, :width] = jnp.concatenate((out_tok[at], out_cot[at]), axis=0).astype(bf16)
        send_a[e, :, width:] = jnp.concatenate((prob_tile[at], prob_tile[at]), axis=0).astype(bf16)

    pl.semaphore_wait(barrier, groups + lanes - 2)

    def a_copy(to, slot):
        return pltpu.make_async_remote_copy(
            src_ref=send_a.at[to],
            dst_ref=recv_a.at[slot],
            send_sem=sa_sem.at[to],
            recv_sem=ra_sem.at[slot],
            device_id=(to, l_me),
            device_id_type=MESH,
        )

    for g in grp_peers:
        a_copy(g, g_me).start()
    recv_a[g_me] = send_a[g_me]
    for load in loads:
        load.wait()
    for g in grp_peers:
        a_copy(g, g).wait_recv()

    tok_in, cot_in, prob_in = [], [], []
    for g in range(groups):
        both = recv_a[g].astype(f32)
        tok_in.append(both[:MOST, :width])
        cot_in.append(both[MOST:, :width])
        prob_in.append(both[:MOST, width:])
    rows_tok = jnp.concatenate(tok_in, axis=0).astype(bf16)
    rows_cot = jnp.concatenate(cot_in, axis=0).astype(bf16)
    prob = jnp.concatenate(prob_in, axis=0)

    def rs_copy(to, slot):
        return pltpu.make_async_remote_copy(
            src_ref=send_rs.at[to],
            dst_ref=recv_rs.at[slot],
            send_sem=ss_sem.at[to],
            recv_sem=rs_sem.at[slot],
            device_id=(g_me, to),
            device_id_type=MESH,
        )

    chips = lanes // 2
    chip_me, core_me = l_me // 2, l_me % 2
    for j in range(1, chips + 1):
        chip = lax.rem(chip_me + j, chips)
        at = pl.ds(pl.multiple_of(chip * (2 * chunk), 2 * chunk), 2 * chunk)
        parts = (
            jnp.dot(rows_tok, wg[:, at], preferred_element_type=f32).astype(bf16),
            jnp.dot(rows_tok, wu[:, at], preferred_element_type=f32).astype(bf16),
            nt_dot(rows_cot, wd[at, :]).astype(bf16),
        )
        for h in range(2):
            for i, part in enumerate(parts):
                send_rs[2 * chip + h, :, i * chunk : (i + 1) * chunk] = part[
                    :, h * chunk : (h + 1) * chunk
                ]
            if j < chips:
                rs_copy(2 * chip + h, l_me).start()
    rs_copy(2 * chip_me + 1 - core_me, l_me).start()
    recv_rs[l_me] = send_rs[l_me]
    for l in lane_peers:
        rs_copy(l, l).wait_recv()

    summed = recv_rs[0].astype(f32)
    for l in range(1, lanes):
        summed = summed + recv_rs[l].astype(f32)
    gate, upward, grad = (summed[:, i * chunk : (i + 1) * chunk] for i in range(3))
    sig = jax.nn.sigmoid(gate)
    act = gate * sig
    slope = sig * (1.0 + gate * (1.0 - sig))
    hidden = act * upward
    dpart = jnp.sum(hidden * grad, axis=1, keepdims=True)
    dhid = prob * grad
    gat[l_me, :, :chunk] = (dhid * upward * slope).astype(bf16)
    gat[l_me, :, chunk:] = (dhid * act).astype(bf16)
    late[l_me, :, :chunk] = (prob * hidden).astype(bf16)
    high = dpart.astype(bf16).astype(f32)
    lane_id = lax.broadcasted_iota(jnp.int32, (rows, chunk), 1)
    late[l_me, :, chunk:] = jnp.where(lane_id < chunk // 2, high, dpart - high).astype(bf16)

    def ag_copy(buf, sent, got, to, slot):
        return pltpu.make_async_remote_copy(
            src_ref=buf.at[slot],
            dst_ref=buf.at[slot],
            send_sem=sent.at[to],
            recv_sem=got.at[slot],
            device_id=(g_me, to),
            device_id_type=MESH,
        )

    for l in lane_peers:
        ag_copy(gat, sg_sem, rg_sem, l, l_me).start()
    for l in lane_peers:
        ag_copy(late, sl_sem, rl_sem, l, l_me).start()

    contrib = jnp.zeros((rows, width), f32)
    for j in range(chips):
        chip = lax.rem(chip_me + j, chips)
        if j == 0:
            mate = 2 * chip_me + 1 - core_me
            ag_copy(gat, sg_sem, rg_sem, mate, mate).wait_recv()
        else:
            for h in range(2):
                l = 2 * chip + h
                ag_copy(gat, sg_sem, rg_sem, l, l).wait_recv()
        at = pl.ds(pl.multiple_of(chip * (2 * chunk), 2 * chunk), 2 * chunk)
        one, two = gat[2 * chip], gat[2 * chip + 1]
        pair_gate = jnp.concatenate((one[:, :chunk], two[:, :chunk]), axis=1)
        pair_up = jnp.concatenate((one[:, chunk:], two[:, chunk:]), axis=1)
        contrib = contrib + nt_dot(pair_gate, wg[:, at]) + nt_dot(pair_up, wu[:, at])

    for l in lane_peers:
        ag_copy(late, sl_sem, rl_sem, l, l).wait_recv()
    d_gate = jnp.concatenate([gat[l, :, :chunk] for l in range(lanes)], axis=1)
    d_up = jnp.concatenate([gat[l, :, chunk:] for l in range(lanes)], axis=1)
    scaled = jnp.concatenate([late[l, :, :chunk] for l in range(lanes)], axis=1)
    dtile = late[0, :, chunk:].astype(f32)
    for l in range(1, lanes):
        dtile = dtile + late[l, :, chunk:].astype(f32)
    dprob = jnp.sum(dtile, axis=1, keepdims=True) * (2.0 / chunk)
    dprob = jnp.broadcast_to(dprob, (rows, 128))

    for e in range(groups):
        at = slice(e * MOST, (e + 1) * MOST)
        right = jnp.concatenate((contrib[at, left:], dprob[at]), axis=1)
        pad = left - right.shape[1]
        if pad:
            right = jnp.concatenate((right, jnp.zeros((MOST, pad), f32)), axis=1)
        send_b[e] = jnp.concatenate((contrib[at, :left], right), axis=0).astype(bf16)

    def b_copy(to, slot):
        return pltpu.make_async_remote_copy(
            src_ref=send_b.at[to],
            dst_ref=recv_b.at[slot],
            send_sem=sb_sem.at[to],
            recv_sem=rb_sem.at[slot],
            device_id=(to, l_me),
            device_id_type=MESH,
        )

    for g in grp_peers:
        b_copy(g, g_me).start()
    recv_b[g_me] = send_b[g_me]

    tok_t_ref[...] = rows_tok.astype(f32).T.astype(bf16)
    sc_t_ref[...] = scaled.astype(f32).T.astype(bf16)
    cot_rows_ref[...] = rows_cot
    d_gate_ref[...] = d_gate
    d_up_ref[...] = d_up

    for g in grp_peers:
        b_copy(g, g).wait_recv()
    low, top = [], []
    for g in range(groups):
        both = recv_b[g].astype(f32)
        low.append(both[:MOST])
        top.append(both[MOST:])
    low = jnp.concatenate(low, axis=0).astype(bf16)
    top = jnp.concatenate(top, axis=0).astype(bf16)
    back = placer_t.astype(bf16)
    tg_ref[:, :left] = jnp.dot(back, low, preferred_element_type=f32).astype(bf16)
    tg_ref[:, left:] = jnp.dot(
        back, top[:, : width - left], preferred_element_type=f32
    ).astype(bf16)
    dback = top[:, width - left : width - left + 128]
    for k in range(fanout):
        mine = jnp.dot((placer_t * hits[k]).astype(bf16), dback, preferred_element_type=f32)
        lane_row = jnp.sum(jnp.where(eye, mine[:, :1], 0.0), axis=0, keepdims=True)
        pg_ref[k : k + 1, :] = lane_row

    for g in grp_peers:
        a_copy(g, g_me).wait_send()
        b_copy(g, g_me).wait_send()
    for l in lane_peers:
        rs_copy(l, l_me).wait_send()
        ag_copy(gat, sg_sem, rg_sem, l, l_me).wait_send()
        ag_copy(late, sl_sem, rl_sem, l, l_me).wait_send()


def outer(tg_in, pg_in, tok_t, sc_t, cot_rows, d_gate, d_up, tg, pg, gg, ug, dg):
    f32, bf16 = jnp.float32, jnp.bfloat16

    @pl.when(pl.program_id(0) == 0)
    def _():
        tg[...] = tg_in[...]
        pg[...] = pg_in[...].astype(bf16)

    gg[0] = jnp.dot(tok_t[...], d_gate[...], preferred_element_type=f32).astype(bf16)
    ug[0] = jnp.dot(tok_t[...], d_up[...], preferred_element_type=f32).astype(bf16)
    dg[0] = jnp.dot(sc_t[...], cot_rows[...], preferred_element_type=f32).astype(bf16)


def shards(tokens, grad_out, routes, route_probs, gate_weight, up_weight, down_weight):
    groups = lax.axis_size("grp")
    lanes = lax.axis_size("lane")
    tok_rows, width = tokens.shape
    units = gate_weight.shape[2]
    chunk = units // lanes
    args = (tokens, grad_out, routes, route_probs, gate_weight, up_weight, down_weight)
    if width % 128 or chunk % 128 or lanes % 2 or tok_rows % 16:
        return plain_shards(*args)
    rows = groups * MOST
    left = 128 * ((width // 128 + 2) // 2)
    bf16 = jnp.bfloat16
    vmem = pl.BlockSpec(memory_space=pltpu.VMEM)
    hbm = pl.BlockSpec(memory_space=pltpu.HBM)
    dma = pltpu.SemaphoreType.DMA
    fanout = routes.shape[1]
    token_grad, prob_grad, tok_t, sc_t, cot_rows, d_gate, d_up = pl.pallas_call(
        functools.partial(fused, groups, lanes),
        out_shape=(
            jax.ShapeDtypeStruct(tokens.shape, bf16),
            jax.ShapeDtypeStruct((fanout, tok_rows), jnp.float32),
            jax.ShapeDtypeStruct((width, rows), bf16),
            jax.ShapeDtypeStruct((units, rows), bf16),
            jax.ShapeDtypeStruct((rows, width), bf16),
            jax.ShapeDtypeStruct((rows, units), bf16),
            jax.ShapeDtypeStruct((rows, units), bf16),
        ),
        in_specs=[vmem] * 2 + [hbm] * 5,
        out_specs=(vmem,) * 7,
        scratch_shapes=[
            pltpu.VMEM((tok_rows, width), bf16),
            pltpu.VMEM((tok_rows, width), bf16),
            pltpu.VMEM((width, units), bf16),
            pltpu.VMEM((width, units), bf16),
            pltpu.VMEM((units, width), bf16),
            pltpu.VMEM((groups, 2 * MOST, width + chunk), bf16),
            pltpu.VMEM((groups, 2 * MOST, width + chunk), bf16),
            pltpu.VMEM((lanes, rows, 3 * chunk), bf16),
            pltpu.VMEM((lanes, rows, 3 * chunk), bf16),
            pltpu.VMEM((lanes, rows, 2 * chunk), bf16),
            pltpu.VMEM((lanes, rows, 2 * chunk), bf16),
            pltpu.VMEM((groups, 2 * MOST, left), bf16),
            pltpu.VMEM((groups, 2 * MOST, left), bf16),
            dma((5,)),
            dma((groups,)),
            dma((groups,)),
            dma((lanes,)),
            dma((lanes,)),
            dma((lanes,)),
            dma((lanes,)),
            dma((lanes,)),
            dma((lanes,)),
            dma((groups,)),
            dma((groups,)),
        ],
        compiler_params=pltpu.CompilerParams(
            collective_id=0, has_side_effects=True, vmem_limit_bytes=58 * 1024 * 1024
        ),
    )(routes.T, route_probs.T, tokens, grad_out, gate_weight, up_weight, down_weight)
    steps = 4
    wide, tall = units // steps, units // steps
    whole = lambda *shape: pl.BlockSpec(shape, lambda i: (0,) * len(shape))
    token_grad, prob_grad, gate_grad, up_grad, down_grad = pl.pallas_call(
        outer,
        grid=(steps,),
        out_shape=(
            jax.ShapeDtypeStruct(tokens.shape, bf16),
            jax.ShapeDtypeStruct((fanout, tok_rows), bf16),
            jax.ShapeDtypeStruct(gate_weight.shape, bf16),
            jax.ShapeDtypeStruct(up_weight.shape, bf16),
            jax.ShapeDtypeStruct(down_weight.shape, bf16),
        ),
        in_specs=[
            whole(tok_rows, width),
            whole(fanout, tok_rows),
            whole(width, rows),
            pl.BlockSpec((tall, rows), lambda i: (i, 0)),
            whole(rows, width),
            pl.BlockSpec((rows, wide), lambda i: (0, i)),
            pl.BlockSpec((rows, wide), lambda i: (0, i)),
        ],
        out_specs=(
            whole(tok_rows, width),
            whole(fanout, tok_rows),
            pl.BlockSpec((1, width, wide), lambda i: (0, 0, i)),
            pl.BlockSpec((1, width, wide), lambda i: (0, 0, i)),
            pl.BlockSpec((1, tall, width), lambda i: (0, i, 0)),
        ),
        compiler_params=pltpu.CompilerParams(vmem_limit_bytes=58 * 1024 * 1024),
    )(token_grad, prob_grad, tok_t, sc_t, cot_rows, d_gate, d_up)
    return token_grad, prob_grad.T, gate_grad, up_grad, down_grad


def solution(mesh):
    placed = (
        P("grp", "lane"),
        P("grp", "lane"),
        P("grp", None),
        P("grp", None),
        P("grp", "lane", None),
        P("grp", "lane", None),
        P("grp", None, "lane"),
    )
    return jax.shard_map(
        shards,
        mesh=mesh,
        in_specs=placed,
        out_specs=(
            P("grp", "lane"),
            P("grp", None),
            P("grp", "lane", None),
            P("grp", "lane", None),
            P("grp", None, "lane"),
        ),
        check_vma=False,
    )
```
